32 devices in a mesh: lat: 8 (over z, x), chan: 4 (over y, core).
Axes of the slice: x: 2, y: 2, z: 4, core: 2. Of those that a mesh axis runs over, the one named last changes fastest.
Arguments:
- probe_field: bfloat16 [2, 384, 384, 1024], P(None, 'lat', 'chan'), may hold values from -6 to 6
- gate_slope: bfloat16 [384, 768, 1024], P('lat', None, 'chan'), may hold values from -0.099609375 to 1.09375
- spectral_filter: float32 [384, 384], P(None, 'chan'), may hold values from -4 to 4
- weight_in: bfloat16 [384, 768], replicated, may hold values from -0.3125 to 0.3125
- weight_out: bfloat16 [768, 384], replicated, may hold values from -0.21875 to 0.21875
- weight_flux: bfloat16 [384, 4], replicated, may hold values from -0.3125 to 0.3125
- send_cells: int32 [32, 8, 128], P(('lat', 'chan')), may hold values from 0 to 12287
- recv_slots: int32 [32, 4, 2048], P(('lat', 'chan')), may hold values from 0 to 1023
- recv_weights: float32 [32, 4, 2048], P(('lat', 'chan')), may hold values from 0.1 to 0.5
- ocean_probe: bfloat16 [2, 200, 64, 1024], P(None, None, 'lat', 'chan'), may hold values from -6 to 6
- ocean_mask: int32 [64, 1024], P('lat', 'chan'), may hold values 0 or 1
- coupling: bfloat16 [4, 200], replicated, may hold values from -3 to 3
- base_fine: bfloat16 [200, 64, 1024], P(None, 'lat', 'chan'), may hold values from -5 to 5
- sigma_fine: float32 [64, 1024], P('lat', 'chan'), may hold values from 0.5 to 2
- slope_fine: bfloat16 [800, 64, 1024], P(None, 'lat', 'chan'), may hold values from -0.099609375 to 1.09375
- gain_fine: float32 [200], replicated, may hold values from 0.1 to 1.9
- kernel_fine: float32 [200, 49], replicated, may hold values from -0.875 to 0.875
- expand_fine: bfloat16 [200, 800], replicated, may hold values from -0.4375 to 0.4375
- shrink_fine: bfloat16 [800, 200], replicated, may hold values from -0.21875 to 0.21875
- down_proj: bfloat16 [200, 250], replicated, may hold values from -0.4375 to 0.4375
- base_coarse: bfloat16 [250, 32, 512], P(None, 'lat', 'chan'), may hold values from -5 to 5
- sigma_coarse: float32 [32, 512], P('lat', 'chan'), may hold values from 0.5 to 2
- slope_coarse: bfloat16 [1000, 32, 512], P(None, 'lat', 'chan'), may hold values from -0.099609375 to 1.09375
- gain_coarse: float32 [250], replicated, may hold values from 0.1 to 1.9
- kernel_coarse: float32 [250, 49], replicated, may hold values from -0.875 to 0.875
- expand_coarse: bfloat16 [250, 1000], replicated, may hold values from -0.375 to 0.375
- shrink_coarse: bfloat16 [1000, 250], replicated, may hold values from -0.1875 to 0.1875
- up_proj: bfloat16 [250, 200], replicated, may hold values from -0.375 to 0.375
Outputs:
- atmos_out: bfloat16 [2, 384, 384, 1024], P(None, 'lat', 'chan')
- ocean_out: bfloat16 [2, 200, 64, 1024], P(None, None, 'lat', 'chan')
The draws below stay inside these ranges and needn't reach their ends.
Inputs may be any that keep to these rules, and one draw needn't show every extreme that they name: `send_cells`: local cell numbers of a flux tile of 48 by 256 cells. `recv_slots`: slot numbers into the 8 times 128 received cells.
All inputs are finite; a program needn't handle non-finite values. No bound on the sum of `ocean_mask` on one device may be relied on, other than what follows from the above.
Results may differ from the reference program's by a relative error of at most 0.023.
Values may be sent and summed in bfloat16 or wider, within the bound.
No kernel may reach another device: no remote copies, remote signals or barrier semaphores. Data moves between devices by JAX's collectives and lax.ppermute only.
A program may use at most 256 MiB of HBM per device.

```python
import math
import jax
import jax.numpy as jnp
from jax import lax

PROBES = 2
NLAT = 384
NLON = 1024
C = 384
HID = 768
FLUX = 4
CAP = 128
KSRC = 4
OY = 8
OX = 256
OCH1 = 200
OCH2 = 250
LAT_DEV = 48
LON_DEV = 256
OYT = 64
OXT = 1024
OCELLS = 2048
N_LAT = 8
N_CHAN = 4


def plant(drawn, own_key, low, largest):
    longest = drawn.shape.index(max(drawn.shape))
    spots = []
    for shift in (0, 1):
        where = [jax.random.randint(jax.random.fold_in(own_key, axis), (), 0, length) for axis, length in enumerate(drawn.shape)]
        where[longest] = (where[longest] + shift) % drawn.shape[longest]
        spots.append(tuple(where))
    return drawn.at[spots[0]].set(low).at[spots[1]].set(largest)


def shard_levels(rng, shape, cuts, smallest, high):
    loudness = 1.0
    for dim, blocks in cuts:
        steps = jax.random.uniform(jax.random.fold_in(jax.random.fold_in(rng, 6), dim), (blocks,), jnp.float32, smallest / len(cuts), high / len(cuts))
        loudness = loudness * jnp.repeat(jnp.exp(steps), shape[dim] // blocks).reshape((-1,) + (1,) * (len(shape) - 1 - dim))
    return loudness


def scatter_about(rng, dims, scale, limit, split=(), kind=jnp.bfloat16):
    entries = scale * jax.random.normal(rng, dims, jnp.float32)
    if split:
        entries = entries * shard_levels(rng, dims, split, -0.22, 0.18)
    return jnp.clip(entries, -limit, limit).astype(kind)


def setup_inputs(seed: int = 0) -> dict:
    keys = jax.random.split(jax.random.key(seed), 29)
    return {
        "probe_field": scatter_about(keys[0], (PROBES, NLAT, C, NLON), 1.0, 6.0, ((1, 8), (2, 4))),
        "gate_slope": jnp.clip(-0.099609375 + 1.1933594 * jax.random.uniform(keys[1], (NLAT, HID, NLON), jnp.float32) ** shard_levels(keys[1], (NLAT, HID, NLON), ((0, 8), (2, 4)), -0.2, 0.2), -0.099609375, 1.09375).astype(jnp.bfloat16),
        "spectral_filter": scatter_about(keys[2], (NLAT, C), 1.0, 4.0, ((1, 4),), jnp.float32),
        "weight_in": scatter_about(keys[3], (C, HID), C ** -0.5, 0.3125),
        "weight_out": scatter_about(keys[4], (HID, C), HID ** -0.5, 0.21875),
        "weight_flux": scatter_about(keys[5], (C, FLUX), C ** -0.5, 0.3125),
        "send_cells": plant(jax.random.randint(keys[6], (N_LAT * N_CHAN, N_LAT, CAP), 0, LAT_DEV * LON_DEV), jax.random.fold_in(keys[6], 1), 0, (LAT_DEV * LON_DEV) - 1).astype(jnp.int32),
        "recv_slots": plant(jax.random.randint(keys[7], (N_LAT * N_CHAN, KSRC, OCELLS), 0, N_LAT * CAP), jax.random.fold_in(keys[7], 1), 0, (N_LAT * CAP) - 1).astype(jnp.int32),
        "recv_weights": jnp.clip(0.1 + 0.4 * jax.random.uniform(keys[8], (N_LAT * N_CHAN, KSRC, OCELLS), jnp.float32) ** shard_levels(keys[8], (N_LAT * N_CHAN, KSRC, OCELLS), ((0, 32),), -0.2, 0.2), 0.1, 0.5),
        "ocean_probe": scatter_about(keys[9], (PROBES, OCH1, OYT, OXT), 1.0, 6.0, ((2, 8), (3, 4))),
        "ocean_mask": plant((jax.random.randint(keys[10], (OYT, OXT), 0, 10) < 7).astype(jnp.int32), jax.random.fold_in(keys[10], 1), 0, 1),
        "coupling": scatter_about(keys[11], (FLUX, OCH1), FLUX ** -0.5, 3.0),
        "base_fine": scatter_about(keys[12], (OCH1, OYT, OXT), 1.0, 5.0, ((1, 8), (2, 4))),
        "sigma_fine": jnp.clip(jnp.exp(math.log(2.0) - 1.3862944 * jax.random.uniform(keys[13], (OYT, OXT), jnp.float32) ** shard_levels(keys[13], (OYT, OXT), ((0, 8), (1, 4)), -0.2, 0.2)), 0.5, 2.0),
        "slope_fine": jnp.clip(-0.099609375 + 1.1933594 * jax.random.uniform(keys[14], (4 * OCH1, OYT, OXT), jnp.float32) ** shard_levels(keys[14], (4 * OCH1, OYT, OXT), ((1, 8), (2, 4)), -0.2, 0.2), -0.099609375, 1.09375).astype(jnp.bfloat16),
        "gain_fine": jnp.clip(1.0 + 0.18 * jax.random.normal(keys[15], (OCH1,), jnp.float32), 0.1, 1.9),
        "kernel_fine": scatter_about(keys[16], (OCH1, 49), 49 ** -0.5, 0.875, (), jnp.float32),
        "expand_fine": scatter_about(keys[17], (OCH1, 4 * OCH1), OCH1 ** -0.5, 0.4375),
        "shrink_fine": scatter_about(keys[18], (4 * OCH1, OCH1), (4 * OCH1) ** -0.5, 0.21875),
        "down_proj": scatter_about(keys[19], (OCH1, OCH2), OCH1 ** -0.5, 0.4375),
        "base_coarse": scatter_about(keys[20], (OCH2, OYT // 2, OXT // 2), 1.0, 5.0, ((1, 8), (2, 4))),
        "sigma_coarse": jnp.clip(jnp.exp(math.log(2.0) - 1.3862944 * jax.random.uniform(keys[21], (OYT // 2, OXT // 2), jnp.float32) ** shard_levels(keys[21], (OYT // 2, OXT // 2), ((0, 8), (1, 4)), -0.2, 0.2)), 0.5, 2.0),
        "slope_coarse": jnp.clip(-0.099609375 + 1.1933594 * jax.random.uniform(keys[22], (4 * OCH2, OYT // 2, OXT // 2), jnp.float32) ** shard_levels(keys[22], (4 * OCH2, OYT // 2, OXT // 2), ((1, 8), (2, 4)), -0.2, 0.2), -0.099609375, 1.09375).astype(jnp.bfloat16),
        "gain_coarse": jnp.clip(1.0 + 0.18 * jax.random.normal(keys[23], (OCH2,), jnp.float32), 0.1, 1.9),
        "kernel_coarse": scatter_about(keys[24], (OCH2, 49), 49 ** -0.5, 0.875, (), jnp.float32),
        "expand_coarse": scatter_about(keys[25], (OCH2, 4 * OCH2), OCH2 ** -0.5, 0.375),
        "shrink_coarse": scatter_about(keys[26], (4 * OCH2, OCH2), (4 * OCH2) ** -0.5, 0.1875),
        "up_proj": scatter_about(keys[27], (OCH2, OCH1), OCH2 ** -0.5, 0.375),
    }


def fourier_tables(count):
    column = jnp.arange(count, dtype=jnp.int32)
    half = count // 2
    wave = jnp.where(column <= half, column, column - half)
    points = jnp.arange(count, dtype=jnp.int32)
    phase = (points[:, None] * wave[None, :]) % count
    angles = phase.astype(jnp.float32) * (2.0 * math.pi / count)
    basis = jnp.where((column <= half)[None, :], jnp.cos(angles), jnp.sin(angles))
    forward = (basis / count).astype(jnp.bfloat16)
    factor = jnp.where((column == 0) | (column == half), 1.0, 2.0).astype(jnp.float32)
    inverse = (basis.T * factor[:, None]).astype(jnp.bfloat16)
    return forward, inverse


def cosine_tables(count):
    degree = jnp.arange(count, dtype=jnp.int32)
    points = jnp.arange(count, dtype=jnp.int32)
    phase = (degree[None, :] * (2 * points[:, None] + 1)) % (4 * count)
    basis = jnp.cos(phase.astype(jnp.float32) * (math.pi / (2 * count)))
    forward = (basis / count).astype(jnp.bfloat16)
    factor = jnp.where(degree == 0, 1.0, 2.0).astype(jnp.float32)
    inverse = (basis.T * factor[:, None]).astype(jnp.bfloat16)
    return forward, inverse


def atmosphere_step(field, gate_slope, spectral_filter, weight_in, weight_out, weight_flux):
    fwd_lon, inv_lon = fourier_tables(NLON)
    fwd_lat, inv_lat = cosine_tables(NLAT)
    fourier = jnp.einsum('ncx,xk->nkc', field.astype(jnp.float32), fwd_lon.astype(jnp.float32)).astype(jnp.bfloat16)
    spectrum = jnp.einsum('nkc,nl->lkc', fourier.astype(jnp.float32), fwd_lat.astype(jnp.float32))
    filtered = (spectrum * spectral_filter[:, None, :]).astype(jnp.bfloat16)
    returned = jnp.einsum('lkc,ln->nkc', filtered.astype(jnp.float32), inv_lat.astype(jnp.float32)).astype(jnp.bfloat16)
    spatial = jnp.einsum('nkc,kx->ncx', returned.astype(jnp.float32), inv_lon.astype(jnp.float32))
    mixed = (field.astype(jnp.float32) + spatial).astype(jnp.bfloat16)

    def row_step(parts):
        mix_row, slope_row, field_row = parts
        hidden = jnp.dot(weight_in.T, mix_row, preferred_element_type=jnp.float32)
        gated = (slope_row.astype(jnp.float32) * hidden).astype(jnp.bfloat16)
        update = jnp.dot(weight_out.T, gated, preferred_element_type=jnp.float32).astype(jnp.bfloat16)
        result = field_row.astype(jnp.float32) + update.astype(jnp.float32)
        flux_row = jnp.dot(weight_flux.T.astype(jnp.float32), result, precision=lax.Precision.HIGHEST)
        return result.astype(jnp.bfloat16), flux_row.astype(jnp.bfloat16)

    output, flux = lax.map(row_step, (mixed, gate_slope, field))
    return output, jnp.transpose(flux, (1, 0, 2))


def route_fluxes(flux, send_cells, recv_slots, recv_weights):
    tiles = flux.reshape(PROBES, FLUX, N_LAT, LAT_DEV, N_CHAN, LON_DEV)
    tiles = tiles.transpose(2, 4, 0, 1, 3, 5).reshape(N_LAT * N_CHAN, PROBES, FLUX, LAT_DEV * LON_DEV)

    def pick(source, cells):
        return jnp.take(source, cells.reshape(-1), axis=2).reshape(PROBES, FLUX, N_LAT, CAP)

    sent = jax.vmap(pick)(tiles, send_cells).reshape(N_LAT, N_CHAN, PROBES, FLUX, N_LAT, CAP)
    received = sent.transpose(4, 1, 2, 3, 0, 5).reshape(N_LAT * N_CHAN, PROBES, FLUX, N_LAT * CAP)

    def combine(buffer, slot_ids, weights):
        taken = jnp.take(buffer, slot_ids.reshape(-1), axis=2).reshape(PROBES, FLUX, KSRC, OCELLS)
        return jnp.sum(taken.astype(jnp.float32) * weights[None, None], axis=2)

    ocean_flux = jax.vmap(combine)(received, recv_slots, recv_weights)
    ocean_flux = ocean_flux.reshape(N_LAT, N_CHAN, PROBES, FLUX, OY, OX).transpose(2, 3, 0, 4, 1, 5)
    return ocean_flux.reshape(PROBES, FLUX, OYT, OXT)


def depthwise(padded, kernel, rows, cols):
    total = jnp.zeros((padded.shape[0], padded.shape[1], rows, cols), jnp.float32)
    wide = padded.astype(jnp.float32)
    for offset in range(49):
        row_start = offset // 7
        col_start = offset % 7
        total = total + wide[:, :, row_start:row_start + rows, col_start:col_start + cols] * kernel[:, offset][None, :, None, None]
    return total


def level_tangent(field, base, sigma, slope, gain, kernel, expand, shrink, mask_values):
    rows = field.shape[2]
    cols = field.shape[3]
    padded = jnp.pad(field, ((0, 0), (0, 0), (3, 3), (3, 3)))
    spread = depthwise(padded, kernel, rows, cols)
    center = jnp.mean(spread, axis=1, keepdims=True)
    normed = base.astype(jnp.float32)[None]
    along = jnp.mean(normed * spread, axis=1, keepdims=True)
    tangent = (gain[None, :, None, None] * sigma[None, None] * (spread - center - normed * along)).astype(jnp.bfloat16)
    hidden = jnp.einsum('pqyx,qh->phyx', tangent.astype(jnp.float32), expand.astype(jnp.float32))
    gated = (slope.astype(jnp.float32)[None] * hidden).astype(jnp.bfloat16)
    output = jnp.einsum('phyx,hq->pqyx', gated.astype(jnp.float32), shrink.astype(jnp.float32))
    return ((field.astype(jnp.float32) + output) * mask_values).astype(jnp.bfloat16)


def reference(probe_field, gate_slope, spectral_filter, weight_in, weight_out, weight_flux, send_cells, recv_slots, recv_weights, ocean_probe, ocean_mask, coupling, base_fine, sigma_fine, slope_fine, gain_fine, kernel_fine, expand_fine, shrink_fine, down_proj, base_coarse, sigma_coarse, slope_coarse, gain_coarse, kernel_coarse, expand_coarse, shrink_coarse, up_proj):
    def probe_step(field):
        return atmosphere_step(field, gate_slope, spectral_filter, weight_in, weight_out, weight_flux)

    atmos_out, flux = lax.map(probe_step, probe_field)
    ocean_flux = route_fluxes(flux, send_cells, recv_slots, recv_weights)
    mask_values = ocean_mask.astype(jnp.float32)

    def ocean_step(pair):
        probe_one = pair[0][None]
        flux_one = pair[1][None]
        forcing = jnp.einsum('pfyx,fq->pqyx', flux_one, coupling.astype(jnp.float32), precision=lax.Precision.HIGHEST)
        start_field = ((probe_one.astype(jnp.float32) + forcing) * mask_values).astype(jnp.bfloat16)
        level_one = level_tangent(start_field, base_fine, sigma_fine, slope_fine, gain_fine, kernel_fine, expand_fine, shrink_fine, mask_values)
        shaped = level_one.astype(jnp.float32).reshape(1, OCH1, OYT // 2, 2, OXT // 2, 2)
        pooled = jnp.mean(shaped, axis=(3, 5))
        coarse_field = jnp.einsum('pqyx,qr->pryx', pooled, down_proj.astype(jnp.float32), precision=lax.Precision.HIGHEST).astype(jnp.bfloat16)
        level_two = level_tangent(coarse_field, base_coarse, sigma_coarse, slope_coarse, gain_coarse, kernel_coarse, expand_coarse, shrink_coarse, 1.0)
        raised = jnp.einsum('pryx,rq->pqyx', level_two.astype(jnp.float32), up_proj.astype(jnp.float32))
        upsampled = jnp.repeat(jnp.repeat(raised, 2, axis=2), 2, axis=3)
        return ((level_one.astype(jnp.float32) + upsampled) * mask_values).astype(jnp.bfloat16)[0]

    ocean_out = lax.map(ocean_step, (ocean_probe, ocean_flux))
    return atmos_out, ocean_out
```

```python
import functools
import math

import jax
import jax.numpy as jnp
from jax import lax
from jax.experimental import pallas as pl
from jax.experimental.pallas import tpu as pltpu
from jax.sharding import PartitionSpec as P

BF16 = jnp.bfloat16
F32 = jnp.float32
VMEM_BYTES = 56 * 1024 * 1024


def whole_spec(array):
    rank = array.ndim
    return pl.BlockSpec(array.shape, lambda *_: (0,) * rank)


def call(body, grid, in_specs, out_specs, out_shape, flops, moved, scratch=(), **extra):
    return pl.pallas_call(
        body,
        grid=grid,
        in_specs=in_specs,
        out_specs=out_specs,
        out_shape=out_shape,
        scratch_shapes=list(scratch),
        compiler_params=pltpu.CompilerParams(vmem_limit_bytes=VMEM_BYTES),
        cost_estimate=pl.CostEstimate(
            flops=int(flops), bytes_accessed=int(moved), transcendentals=0
        ),
        **extra,
    )


def dot(left, right):
    return jnp.dot(left, right, preferred_element_type=F32)


def tie(value, *others):
    others = jax.tree.leaves(others)
    anywhere = pl.BlockSpec(memory_space=pl.ANY)

    def body(*refs):
        pass

    return pl.pallas_call(
        body,
        in_specs=[anywhere] * (1 + len(others)),
        out_specs=anywhere,
        out_shape=jax.ShapeDtypeStruct(value.shape, value.dtype),
        input_output_aliases={0: 0},
        cost_estimate=pl.CostEstimate(flops=0, bytes_accessed=0, transcendentals=0),
    )(value, *others)


def cosine_tables(count):
    degree = jnp.arange(count, dtype=jnp.int32)
    points = jnp.arange(count, dtype=jnp.int32)
    phase = degree[None, :] * (2 * points[:, None] + 1) % (4 * count)
    basis = jnp.cos(phase.astype(F32) * (math.pi / (2 * count)))
    forward = (basis / count).astype(BF16)
    factor = jnp.where(degree == 0, 1.0, 2.0).astype(F32)
    inverse = (basis.T * factor[:, None]).astype(BF16)
    return (forward, inverse)


def with_halo(block, sides, width):
    for axis, dim in sides:
        count = lax.axis_size(axis)
        forward = [(i, i + 1) for i in range(count - 1)]
        backward = [(target, source) for source, target in forward]
        low = lax.ppermute(
            lax.slice_in_dim(block, block.shape[dim] - width, None, axis=dim), axis, forward
        )
        high = lax.ppermute(lax.slice_in_dim(block, 0, width, axis=dim), axis, backward)
        block = jnp.concatenate([low, block, high], axis=dim)
    return block


def mix_kernel(lat_devices, lon_blocks, field_ref, fwd_ref, inv_ref, filter_ref, *out_refs):
    rows, lanes = field_ref.shape[2:]
    width = out_refs[0].shape[3]
    for part, out_ref in enumerate(out_refs):
        starts = [(lon * len(out_refs) + part) * width for lon in range(lon_blocks)]
        block = jnp.concatenate(
            [field_ref[:, 0, :, start : start + width] for start in starts], axis=2
        )
        if rows % 16:
            block = block.astype(F32)
        field = block.reshape(lat_devices * rows, lon_blocks * width).astype(BF16)
        spectrum = dot(fwd_ref[...], field)
        filtered = (spectrum * filter_ref[0]).astype(BF16)
        mixed = field.astype(F32) + dot(inv_ref[...], filtered)
        for band in range(lat_devices):
            for lon in range(lon_blocks):
                out_ref[band * lon_blocks + lon, 0] = mixed[
                    band * rows : (band + 1) * rows, lon * width : (lon + 1) * width
                ].astype(BF16)


def mix_latitudes(gathered, fwd_rows, inv_rows, filters, lon_blocks, parts):
    lat_devices, channels, rows, lanes = gathered.shape
    width = lanes // (lon_blocks * parts)
    count = lat_devices * rows
    peers = lat_devices * lon_blocks
    return call(
        functools.partial(mix_kernel, lat_devices, lon_blocks),
        (channels,),
        [
            pl.BlockSpec((lat_devices, 1, rows, lanes), lambda c: (0, c, 0, 0)),
            whole_spec(fwd_rows),
            whole_spec(inv_rows),
            pl.BlockSpec((1, count, 1), lambda c: (c, 0, 0)),
        ],
        [pl.BlockSpec((peers, 1, rows, width), lambda c: (0, c, 0, 0))] * parts,
        [jax.ShapeDtypeStruct((peers, channels, rows, width), BF16)] * parts,
        4 * count * count * lanes * channels,
        4 * gathered.size,
    )(gathered, fwd_rows, inv_rows, filters)


def network_kernel(mixed_ref, slope_ref, win_ref, wout_ref, wflux_ref, flux_ref, *piece_refs):
    for row in range(mixed_ref.shape[0]):
        hidden = dot(win_ref[...], mixed_ref[row])
        gated = (slope_ref[row].astype(F32) * hidden).astype(BF16)
        update = dot(wout_ref[...], gated).astype(BF16)
        flux_ref[:, row] = dot(wflux_ref[...], update)
        width = piece_refs[0].shape[1]
        for index, piece_ref in enumerate(piece_refs):
            piece_ref[row] = update[index * width : (index + 1) * width]


def network(mixed, slope, part, win, wout, wflux, pieces):
    rows, channels, lanes = mixed.shape
    hidden = slope.shape[1]
    fluxes = wflux.shape[0]
    width = channels // pieces
    step = 8
    return call(
        network_kernel,
        (rows // step,),
        [
            pl.BlockSpec((step, channels, lanes), lambda n: (n, 0, 0)),
            pl.BlockSpec((step, hidden, lanes), lambda n: (n, 0, part)),
            whole_spec(win),
            whole_spec(wout),
            whole_spec(wflux),
        ],
        [pl.BlockSpec((fluxes, step, lanes), lambda n: (0, n, 0))]
        + [pl.BlockSpec((step, width, lanes), lambda n: (n, 0, 0))] * pieces,
        [jax.ShapeDtypeStruct((fluxes, rows, lanes), F32)]
        + [jax.ShapeDtypeStruct((rows, width, lanes), BF16)] * pieces,
        4 * rows * lanes * channels * hidden,
        2 * rows * lanes * (2 * channels + hidden),
    )(mixed, slope, win, wout, wflux)


def finish_kernel(parts, columns, place_ref, field_ref, *refs):
    out_ref = refs[-1]
    lanes = refs[0].shape[2]
    for index in range(parts * columns):
        part, shift = divmod(index, columns)
        block = lax.rem(place_ref[0] - shift + columns, columns)
        start = pl.multiple_of((block * parts + part) * lanes, lanes)
        span = pl.ds(start, lanes)
        out_ref[0, :, :, span] = (
            field_ref[0, :, :, span].astype(F32) + refs[index][...].astype(F32)
        ).astype(BF16)


def finish(probe, place, field, pieces, parts, columns, previous):
    rows, channels, lon_count = field.shape[1:]
    step = 4 if rows % 4 == 0 else 1
    block = pl.BlockSpec((1, step, channels, lon_count), lambda n: (probe, n, 0, 0))
    piece = pl.BlockSpec((step, channels, pieces[0].shape[2]), lambda n: (n, 0, 0))
    operands = [place, field, *pieces]
    specs = [pl.BlockSpec(memory_space=pltpu.SMEM), block] + [piece] * len(pieces)
    extra = {}
    if previous is not None:
        extra["input_output_aliases"] = {len(operands): 0}
        operands.append(previous)
        specs.append(pl.BlockSpec(memory_space=pl.ANY))
    return call(
        functools.partial(finish_kernel, parts, columns),
        (rows // step,),
        specs,
        block,
        jax.ShapeDtypeStruct(field.shape, BF16),
        field.size,
        6 * rows * channels * lon_count,
        **extra,
    )(*operands)


def pick_kernel(row_ref, col_ref, field_ref, *refs):
    part_refs, out_ref = refs[:-1], refs[-1]
    fields, rows, lanes = field_ref.shape
    cells = row_ref.shape[1]
    chosen = lax.broadcasted_iota(jnp.int32, (rows, cells), 0) == row_ref[...]
    chosen = jnp.where(chosen, 1.0, 0.0).astype(BF16)
    column = lax.broadcasted_iota(jnp.int32, (lanes, cells), 0) == col_ref[...]
    for field in range(fields):
        update = jnp.concatenate([part_ref[field] for part_ref in part_refs], axis=1)
        tile = (field_ref[field].astype(F32) + update).astype(BF16)
        lines = lax.dot_general(
            tile, chosen, (((0,), (0,)), ((), ())), preferred_element_type=F32
        )
        picked = jnp.sum(jnp.where(column, lines, 0.0), axis=0, keepdims=True).astype(BF16)
        count = out_ref.shape[2]
        for band in range(out_ref.shape[0]):
            out_ref[band, field : field + 1] = picked[:, band * count : (band + 1) * count]


def pick_cells(row, col, field, parts, bands):
    fields = field.shape[0]
    cells = row.shape[1]
    operands = (row, col, field, *parts)
    return call(
        pick_kernel,
        (1,),
        [whole_spec(operand) for operand in operands],
        pl.BlockSpec((bands, fields, cells // bands), lambda _: (0, 0, 0)),
        jax.ShapeDtypeStruct((bands, fields, cells // bands), BF16),
        4 * field.size * cells,
        8 * field.size,
    )(*operands)


def regrid_kernel(slot_ref, weight_ref, high_ref, low_ref):
    slots = high_ref.shape[1]
    lanes = high_ref.shape[2]
    number = lax.broadcasted_iota(jnp.int32, (slots, lanes), 0)
    total = jnp.zeros((slots, lanes), F32)
    for source in range(slot_ref.shape[1]):
        total = total + jnp.where(
            number == slot_ref[0, source : source + 1], weight_ref[0, source : source + 1], 0.0
        )
    high = total.astype(BF16)
    high_ref[0] = high
    low_ref[0] = (total - high.astype(F32)).astype(BF16)


def regrid_matrix(slot, weight, slots):
    rows, sources, lanes = slot.shape
    line = pl.BlockSpec((1, sources, lanes), lambda y: (y, 0, 0))
    table = pl.BlockSpec((1, slots, lanes), lambda y: (y, 0, 0))
    shape = jax.ShapeDtypeStruct((rows, slots, lanes), BF16)
    return call(
        regrid_kernel,
        (rows,),
        [line, line],
        [table, table],
        [shape, shape],
        12 * rows * slots * lanes,
        4 * rows * slots * lanes,
    )(slot, weight)


def start_kernel(pool_ref, high_ref, low_ref, coupling_ref, probe_ref, mask_ref, out_ref):
    pool = jnp.concatenate([pool_ref[band] for band in range(pool_ref.shape[0])], axis=1)
    flux = dot(pool, high_ref[0]) + dot(pool, low_ref[0])
    coupling = coupling_ref[...]
    total = probe_ref[0].astype(F32)
    for field in range(coupling.shape[1]):
        total = total + coupling[:, field : field + 1] * flux[field : field + 1]
    out_ref[0] = (total * mask_ref[0]).astype(BF16)


def start_level(pool, high, low, coupling, probe, mask):
    rows, channels, lanes = probe.shape
    slots = high.shape[1]
    table = pl.BlockSpec((1, slots, lanes), lambda y: (y, 0, 0))
    line = pl.BlockSpec((1, channels, lanes), lambda y: (y, 0, 0))
    return call(
        start_kernel,
        (rows,),
        [
            whole_spec(pool),
            table,
            table,
            whole_spec(coupling),
            line,
            pl.BlockSpec((1, 1, lanes), lambda y: (y, 0, 0)),
        ],
        line,
        jax.ShapeDtypeStruct(probe.shape, BF16),
        32 * high.size,
        4 * high.size,
    )(pool, high, low, coupling, probe, mask)


def spread_row(padded_ref, taps_ref, spread_ref, row, slot, lanes, chunk):
    channels = taps_ref.shape[1]
    tiles = padded_ref.shape[2] // 128

    def step(index, carry):
        span = pl.ds(pl.multiple_of(index * chunk, chunk), chunk)
        total = jnp.zeros((chunk, lanes), F32)
        for right in range(7):
            sums = [None] * tiles
            for down in range(7):
                tap = taps_ref[down * 7 + right, span, :]
                for tile in range(tiles):
                    term = padded_ref[row + down, span, tile * 128 : (tile + 1) * 128] * tap
                    sums[tile] = term if sums[tile] is None else sums[tile] + term
            line = jnp.concatenate(sums, axis=1)
            total = total + line[:, right : right + lanes]
        spread_ref[slot, span, :] = total
        return carry

    lax.fori_loop(0, channels // chunk, step, 0)


def tangent_row(spread, base, scale, count):
    center = jnp.sum(spread, axis=0, keepdims=True) / count
    along = jnp.sum(base * spread, axis=0, keepdims=True) / count
    return (scale * (spread - center - base * along)).astype(BF16)


def split_dot(left, right):
    high = right.astype(BF16)
    low = (right - high.astype(F32)).astype(BF16)
    return dot(left, high) + dot(left, low)


def fine_kernel(
    padded_ref,
    taps_ref,
    field_ref,
    base_ref,
    sigma_ref,
    slope_ref,
    gain_ref,
    expand_ref,
    shrink_ref,
    down_ref,
    pairs_ref,
    mask_ref,
    level_ref,
    coarse_ref,
    spread_ref,
):
    first = pl.program_id(0) * 2
    channels, lanes = field_ref.shape[1:]
    pooled = None
    for slot in range(2):
        spread_row(padded_ref, taps_ref, spread_ref, first + slot, slot, lanes, 40)
    for slot in range(2):
        tangent = tangent_row(
            spread_ref[slot],
            base_ref[slot].astype(F32),
            gain_ref[...] * sigma_ref[slot],
            channels,
        )
        hidden = dot(expand_ref[...], tangent)
        gated = (slope_ref[slot].astype(F32) * hidden).astype(BF16)
        output = dot(shrink_ref[...], gated)
        level = ((field_ref[slot].astype(F32) + output) * mask_ref[slot]).astype(BF16)
        level_ref[slot] = level
        share = dot(level, pairs_ref[...])
        pooled = share if pooled is None else pooled + share
    coarse_ref[0] = split_dot(down_ref[...], pooled).astype(BF16)


def fine_level(padded, taps, field, base, sigma, slope, gain, expand, shrink, down, pairs, mask):
    rows, channels, lanes = field.shape
    hidden = slope.shape[1]
    wide = down.shape[0]
    line = pl.BlockSpec((2, channels, lanes), lambda y: (y, 0, 0))
    thin = pl.BlockSpec((2, 1, lanes), lambda y: (y, 0, 0))
    return call(
        fine_kernel,
        (rows // 2,),
        [
            whole_spec(padded),
            whole_spec(taps),
            line,
            line,
            thin,
            pl.BlockSpec((2, hidden, lanes), lambda y: (y, 0, 0)),
            whole_spec(gain),
            whole_spec(expand),
            whole_spec(shrink),
            whole_spec(down),
            whole_spec(pairs),
            thin,
        ],
        [line, pl.BlockSpec((1, wide, lanes // 2), lambda y: (y, 0, 0))],
        [
            jax.ShapeDtypeStruct((rows, channels, lanes), BF16),
            jax.ShapeDtypeStruct((rows // 2, wide, lanes // 2), BF16),
        ],
        8 * rows * lanes * channels * hidden,
        4 * padded.size + 4 * taps.size + 2 * slope.size,
        scratch=[pltpu.VMEM((2, channels, lanes), F32)],
    )(padded, taps, field, base, sigma, slope, gain, expand, shrink, down, pairs, mask)


def coarse_kernel(
    count,
    padded_ref,
    taps_ref,
    field_ref,
    base_ref,
    sigma_ref,
    slope_ref,
    gain_ref,
    expand_ref,
    shrink_ref,
    up_ref,
    spread_out_ref,
    level_ref,
    mask_ref,
    out_ref,
    spread_ref,
):
    rows, _, lanes = field_ref.shape
    for row in range(rows):
        spread_row(padded_ref, taps_ref, spread_ref, row, row, lanes, 64)
    tangent = jnp.concatenate(
        [
            tangent_row(
                spread_ref[row],
                base_ref[row].astype(F32),
                gain_ref[...] * sigma_ref[row],
                count,
            )
            for row in range(rows)
        ],
        axis=1,
    )
    hidden = dot(expand_ref[...], tangent)
    gated = jnp.concatenate(
        [
            (slope_ref[row].astype(F32) * hidden[:, row * lanes : (row + 1) * lanes]).astype(BF16)
            for row in range(rows)
        ],
        axis=1,
    )
    output = dot(shrink_ref[...], gated)
    for row in range(rows):
        level = (
            field_ref[row].astype(F32) + output[:, row * lanes : (row + 1) * lanes]
        ).astype(BF16)
        raised = dot(up_ref[...], level)
        high = raised.astype(BF16)
        low = (raised - high.astype(F32)).astype(BF16)
        wide = dot(high, spread_out_ref[...]) + dot(low, spread_out_ref[...])
        for half in range(2):
            line = 2 * row + half
            out_ref[line] = ((level_ref[line].astype(F32) + wide) * mask_ref[line]).astype(BF16)


def coarse_level(
    count, padded, taps, field, base, sigma, slope, gain, expand, shrink, up, copies, level, mask
):
    operands = (
        padded,
        taps,
        field,
        base,
        sigma,
        slope,
        gain,
        expand,
        shrink,
        up,
        copies,
        level,
        mask,
    )
    return call(
        functools.partial(coarse_kernel, count),
        (1,),
        [whole_spec(operand) for operand in operands],
        whole_spec(level),
        jax.ShapeDtypeStruct(level.shape, BF16),
        8 * field.size * slope.shape[1],
        4 * padded.size + 4 * taps.size + 2 * slope.size + 4 * level.size,
        scratch=[pltpu.VMEM(field.shape, F32)],
    )(*operands)


def widen(array, dim, size):
    pads = [(0, 0)] * array.ndim
    pads[dim] = (0, size - array.shape[dim])
    return jnp.pad(array, pads)


def local(
    probe_field,
    gate_slope,
    spectral_filter,
    weight_in,
    weight_out,
    weight_flux,
    send_cells,
    recv_slots,
    recv_weights,
    ocean_probe,
    ocean_mask,
    coupling,
    base_fine,
    sigma_fine,
    slope_fine,
    gain_fine,
    kernel_fine,
    expand_fine,
    shrink_fine,
    down_proj,
    base_coarse,
    sigma_coarse,
    slope_coarse,
    gain_coarse,
    kernel_coarse,
    expand_coarse,
    shrink_coarse,
    up_proj,
):
    probes, rows, width, lon_count = probe_field.shape
    lat_devices = lax.axis_size("lat")
    columns = lax.axis_size("chan")
    lat_place = lax.axis_index("lat")
    place = lax.axis_index("chan")
    channels = width * columns
    group = width // lat_devices
    lon_block = lon_count // columns
    lanes = min(128, lon_block)
    parts = lon_block // lanes
    fluxes = weight_flux.shape[1]

    fwd_lat, inv_lat = cosine_tables(rows * lat_devices)
    fwd_rows, inv_rows = fwd_lat.T, inv_lat.T
    filters = lax.dynamic_slice_in_dim(spectral_filter, lat_place * group, group, 1).T[:, :, None]
    win = (
        weight_in.reshape(columns, lat_devices, group, -1)
        .transpose(3, 1, 0, 2)
        .reshape(-1, channels)
    )
    wout = jnp.roll(weight_out.T, -place * width, axis=0)
    wflux = jnp.roll(weight_flux.T, -place * width, axis=1)
    flux_rows = lax.dynamic_slice_in_dim(weight_flux, place * width, width, 0)

    flux_share = jnp.einsum(
        "pncx,cf->pfnx", probe_field, flux_rows, preferred_element_type=F32
    ).astype(BF16)
    flux_share = flux_share.reshape(probes * fluxes * rows, columns, lon_block).transpose(1, 0, 2)
    flux_field = lax.psum_scatter(flux_share, "chan", scatter_dimension=0, tiled=False)
    flux_field = flux_field.reshape(probes, fluxes, rows, lon_block)

    tile_rows, tile_cols = ocean_probe.shape[2:]
    slots = lat_devices * send_cells.shape[2]
    cells = send_cells.reshape(1, -1)
    cell_row, cell_col = cells // lon_block, cells % lon_block
    sources = recv_slots.shape[1]
    regrid_high, regrid_low = regrid_matrix(
        recv_slots.reshape(sources, tile_rows, tile_cols).transpose(1, 0, 2),
        recv_weights.reshape(sources, tile_rows, tile_cols).transpose(1, 0, 2),
        slots,
    )
    mask = ocean_mask.astype(F32)[:, None, :]
    ocean_start = ocean_probe.transpose(0, 2, 1, 3)
    coupling_rows = coupling.T.astype(F32)
    fine_count = kernel_fine.shape[0]
    coarse_count = kernel_coarse.shape[0]
    wide = -(-coarse_count // 64) * 64
    fine_args = (
        base_fine.transpose(1, 0, 2),
        sigma_fine[:, None, :],
        slope_fine.transpose(1, 0, 2),
        gain_fine[:, None],
        expand_fine.T,
        shrink_fine.T,
        widen(down_proj.T, 0, wide),
    )
    column = jnp.arange(tile_cols)
    pairs = jnp.where(column[:, None] // 2 == jnp.arange(tile_cols // 2)[None, :], 0.25, 0.0)
    pairs = pairs.astype(BF16)
    copies = jnp.where(jnp.arange(tile_cols // 2)[:, None] == column[None, :] // 2, 1.0, 0.0)
    copies = copies.astype(BF16)
    taps_fine = jnp.broadcast_to(kernel_fine.T[:, :, None], (49, fine_count, 128))
    taps_coarse = jnp.broadcast_to(
        widen(kernel_coarse, 0, wide).T[:, :, None], (49, wide, 128)
    )
    coarse_args = (
        widen(base_coarse.transpose(1, 0, 2), 1, wide),
        sigma_coarse[:, None, :],
        slope_coarse.transpose(1, 0, 2),
        widen(gain_coarse[:, None], 0, wide),
        widen(expand_coarse.T, 1, wide),
        widen(shrink_coarse.T, 0, wide),
        widen(up_proj.T, 1, wide),
        copies,
    )

    def send_field(probe):
        block = probe_field[probe].transpose(1, 0, 2)
        return block.reshape(lat_devices, group, rows, lon_count)

    def exchange(block, axes):
        return lax.all_to_all(block, axes, split_axis=0, concat_axis=0, tiled=True)

    def send_update(mixed, part):
        mixed = mixed.reshape(channels, rows, lanes).transpose(1, 0, 2)
        flux, *pieces = network(mixed, gate_slope, part, win, wout, wflux, columns)
        arrived = [pieces[0]]
        for shift in range(1, columns):
            pairs_of = [(source, (source + shift) % columns) for source in range(columns)]
            arrived.append(lax.ppermute(pieces[shift], "chan", pairs_of))
        return flux, arrived

    def ocean_start_field(probe, flux_parts, last):
        picked = pick_cells(cell_row, cell_col, flux_field[probe], flux_parts, lat_devices)
        if last:
            pool = exchange(picked, "lat")
        else:
            pool = lax.all_gather(picked, "lat", axis=0, tiled=False)
            pool = lax.dynamic_index_in_dim(pool, lat_place, 1, keepdims=False)
        return start_level(
            pool, regrid_high, regrid_low, coupling_rows, ocean_start[probe], mask
        )

    def ocean(start):
        padded = with_halo(start, (("lat", 0), ("chan", 2)), 3).astype(F32)
        padded = widen(padded, 2, tile_cols + 128)
        base, sigma, slope, gain, expand, shrink, down = fine_args
        level, coarse = fine_level(
            padded,
            taps_fine,
            start,
            base,
            sigma,
            slope,
            gain,
            expand,
            shrink,
            down,
            pairs,
            mask,
        )
        padded = with_halo(coarse, (("lat", 0), ("chan", 2)), 3).astype(F32)
        padded = widen(padded, 2, tile_cols // 2 + 128)
        return coarse_level(
            coarse_count, padded, taps_coarse, coarse, *coarse_args, level, mask
        )

    place_word = place.astype(jnp.int32).reshape(1)
    prepared = (
        flux_field,
        regrid_high,
        regrid_low,
        mask,
        ocean_start,
        coupling_rows,
        fine_args,
        coarse_args,
        pairs,
        taps_fine,
        taps_coarse,
        win,
        wout,
        wflux,
        cell_row,
        cell_col,
    )
    gathered = []
    for probe in range(probes):
        block = send_field(probe)
        if gathered:
            block = tie(block, gathered[-1], flux_share)
        gathered.append(exchange(block, "lat"))
    mixed = [
        mix_latitudes(block, fwd_rows, inv_rows, filters, columns, parts) for block in gathered
    ]
    order = [(probe, part) for probe in range(probes) for part in range(parts)]
    arrived = []
    updates = []
    starts = []

    def advance(block, *others):
        index = len(updates)
        if others:
            block = tie(block, *others)
        updates.append(send_update(block, order[index][1]))
        if (index + 1) % parts == 0:
            probe = index // parts
            flux_parts = [update[0] for update in updates[probe * parts :]]
            starts.append(ocean_start_field(probe, flux_parts, probe == probes - 1))

    def conclude(probe, previous):
        pieces = [
            piece for update in updates[probe * parts : (probe + 1) * parts] for piece in update[1]
        ]
        result = ocean(starts[probe])
        return result, finish(
            probe, place_word, probe_field, pieces, parts, columns, previous
        )

    for index, (probe, part) in enumerate(order):
        waits = [gathered[-1], prepared] if index == 0 else [arrived[-1]]
        if index == 1:
            waits += [mixed[-1]]
        if index >= 2:
            advance(arrived[index - 2])
            waits += [updates[-1][0], starts[-1:]]
        block = tie(mixed[probe][part], *waits)
        arrived.append(exchange(block, ("lat", "chan")))
    while len(updates) < len(order) - 1:
        advance(arrived[len(updates)])
    results = []
    atmos_out = None
    for probe in range(probes - 1):
        result, atmos_out = conclude(probe, atmos_out)
        results.append(result)
    advance(arrived[-1], results, atmos_out, updates[-1][0])
    result, atmos_out = conclude(probes - 1, atmos_out)
    results.append(result)
    return (atmos_out, jnp.stack(results).transpose(0, 2, 1, 3))


def solution(mesh):
    return jax.shard_map(
        local,
        mesh=mesh,
        in_specs=(
            P(None, "lat", "chan", None),
            P("lat", None, "chan"),
            P(None, "chan"),
            P(),
            P(),
            P(),
            P(("lat", "chan"), None, None),
            P(("lat", "chan"), None, None),
            P(("lat", "chan"), None, None),
            P(None, None, "lat", "chan"),
            P("lat", "chan"),
            P(),
            P(None, "lat", "chan"),
            P("lat", "chan"),
            P(None, "lat", "chan"),
            P(),
            P(),
            P(),
            P(),
            P(),
            P(None, "lat", "chan"),
            P("lat", "chan"),
            P(None, "lat", "chan"),
            P(),
            P(),
            P(),
            P(),
            P(),
        ),
        out_specs=(P(None, "lat", "chan", None), P(None, None, "lat", "chan")),
        check_vma=False,
    )
```

```python
import functools
import math

import jax
import jax.numpy as jnp
from jax import lax
from jax.experimental import pallas as pl
from jax.experimental.pallas import tpu as pltpu
from jax.sharding import PartitionSpec as P

BF16 = jnp.bfloat16
F32 = jnp.float32
VMEM_BYTES = 56 * 1024 * 1024


def whole_spec(array):
    rank = array.ndim
    return pl.BlockSpec(array.shape, lambda *_: (0,) * rank)


def call(body, grid, in_specs, out_specs, out_shape, flops, moved, scratch=(), **extra):
    return pl.pallas_call(
        body,
        grid=grid,
        in_specs=in_specs,
        out_specs=out_specs,
        out_shape=out_shape,
        scratch_shapes=list(scratch),
        compiler_params=pltpu.CompilerParams(vmem_limit_bytes=VMEM_BYTES),
        cost_estimate=pl.CostEstimate(
            flops=int(flops), bytes_accessed=int(moved), transcendentals=0
        ),
        **extra,
    )


def dot(left, right):
    return jnp.dot(left, right, preferred_element_type=F32)


def tie(value, *others):
    others = jax.tree.leaves(others)
    anywhere = pl.BlockSpec(memory_space=pl.ANY)

    def body(*refs):
        pass

    return pl.pallas_call(
        body,
        in_specs=[anywhere] * (1 + len(others)),
        out_specs=anywhere,
        out_shape=jax.ShapeDtypeStruct(value.shape, value.dtype),
        input_output_aliases={0: 0},
        cost_estimate=pl.CostEstimate(flops=0, bytes_accessed=0, transcendentals=0),
    )(value, *others)


def cosine_tables(count):
    degree = jnp.arange(count, dtype=jnp.int32)
    points = jnp.arange(count, dtype=jnp.int32)
    phase = degree[None, :] * (2 * points[:, None] + 1) % (4 * count)
    basis = jnp.cos(phase.astype(F32) * (math.pi / (2 * count)))
    forward = (basis / count).astype(BF16)
    factor = jnp.where(degree == 0, 1.0, 2.0).astype(F32)
    inverse = (basis.T * factor[:, None]).astype(BF16)
    return (forward, inverse)


def shift_from(block, axis, step):
    count = lax.axis_size(axis)
    pairs = [(i, i + step) for i in range(count) if 0 <= i + step < count]
    return lax.ppermute(block, axis, pairs)


def halo_rows(block):
    return shift_from(block[:, -3:], "lat", 1), shift_from(block[:, :3], "lat", -1)


def halo_columns(block, top, bottom):
    def edge(span):
        return jnp.concatenate([piece[..., span] for piece in (top, block, bottom)], axis=1)

    left = shift_from(edge(slice(-3, None)), "chan", 1)
    right = shift_from(edge(slice(0, 3)), "chan", -1)
    return left, right


def turn_kernel(field_ref, out_ref):
    out_ref[...] = jnp.swapaxes(field_ref[0], 0, 1)


def turn(field, probe):
    rows, channels, lon_count = field.shape[1:]
    lanes = 128
    return call(
        turn_kernel,
        (lon_count // lanes,),
        [pl.BlockSpec((1, rows, channels, lanes), lambda x: (probe, 0, 0, x))],
        pl.BlockSpec((channels, rows, lanes), lambda x: (0, 0, x)),
        jax.ShapeDtypeStruct((channels, rows, lon_count), BF16),
        0,
        4 * rows * channels * lon_count,
    )(field)


def mix_kernel(fwd_ref, inv_ref, filter_ref, *refs):
    field_refs, out_ref = refs[:-1], refs[-1]
    lat_devices, channels, rows, width = field_refs[0].shape
    lon_blocks = len(field_refs)
    for channel in range(channels):
        block = jnp.concatenate([field_ref[:, channel] for field_ref in field_refs], axis=2)
        if rows % 16:
            block = block.astype(F32)
        field = block.reshape(lat_devices * rows, lon_blocks * width).astype(BF16)
        spectrum = dot(fwd_ref[...], field)
        filtered = (spectrum * filter_ref[channel]).astype(BF16)
        mixed = field.astype(F32) + dot(inv_ref[...], filtered)
        for band in range(lat_devices):
            for lon in range(lon_blocks):
                out_ref[band * lon_blocks + lon, channel] = mixed[
                    band * rows : (band + 1) * rows, lon * width : (lon + 1) * width
                ].astype(BF16)


def mix_latitudes(gathered, fwd_rows, inv_rows, filters, lon_blocks, part, parts):
    lat_devices, channels, rows, lanes = gathered.shape
    width = lanes // (lon_blocks * parts)
    count = lat_devices * rows
    peers = lat_devices * lon_blocks
    step = 2 if channels % 2 == 0 else 1

    def lines(lon):
        return pl.BlockSpec(
            (lat_devices, step, rows, width), lambda c: (0, c, 0, lon * parts + part)
        )

    return call(
        mix_kernel,
        (channels // step,),
        [
            whole_spec(fwd_rows),
            whole_spec(inv_rows),
            pl.BlockSpec((step, count, 1), lambda c: (c, 0, 0)),
        ]
        + [lines(lon) for lon in range(lon_blocks)],
        pl.BlockSpec((peers, step, rows, width), lambda c: (0, c, 0, 0)),
        jax.ShapeDtypeStruct((peers, channels, rows, width), BF16),
        4 * count * count * lanes * channels // parts,
        4 * gathered.size // parts,
    )(fwd_rows, inv_rows, filters, *([gathered] * lon_blocks))


def network_kernel(mixed_ref, slope_ref, win_ref, wout_ref, wflux_ref, flux_ref, *piece_refs):
    rows, _, lanes = mixed_ref.shape
    width = piece_refs[0].shape[1]
    together = max(1, 256 // lanes)
    for first in range(0, rows, together):
        span = range(first, first + together)
        mixed = jnp.concatenate([mixed_ref[row] for row in span], axis=1)
        slope = jnp.concatenate([slope_ref[row] for row in span], axis=1)
        hidden = dot(win_ref[...], mixed)
        gated = (slope.astype(F32) * hidden).astype(BF16)
        update = dot(wout_ref[...], gated).astype(BF16)
        flux = dot(wflux_ref[...], update)
        for place, row in enumerate(span):
            part = slice(place * lanes, (place + 1) * lanes)
            flux_ref[:, row] = flux[:, part]
            for index, piece_ref in enumerate(piece_refs):
                piece_ref[row] = update[index * width : (index + 1) * width, part]


def network(mixed, slope, part, win, wout, wflux, pieces):
    rows, channels, lanes = mixed.shape
    hidden = slope.shape[1]
    fluxes = wflux.shape[0]
    width = channels // pieces
    step = 8
    return call(
        network_kernel,
        (rows // step,),
        [
            pl.BlockSpec((step, channels, lanes), lambda n: (n, 0, 0)),
            pl.BlockSpec((step, hidden, lanes), lambda n: (n, 0, part)),
            whole_spec(win),
            whole_spec(wout),
            whole_spec(wflux),
        ],
        [pl.BlockSpec((fluxes, step, lanes), lambda n: (0, n, 0))]
        + [pl.BlockSpec((step, width, lanes), lambda n: (n, 0, 0))] * pieces,
        [jax.ShapeDtypeStruct((fluxes, rows, lanes), F32)]
        + [jax.ShapeDtypeStruct((rows, width, lanes), BF16)] * pieces,
        4 * rows * lanes * channels * hidden,
        2 * rows * lanes * (2 * channels + hidden),
    )(mixed, slope, win, wout, wflux)


def finish_kernel(columns, place_ref, field_ref, *refs):
    out_ref = refs[-1]
    for shift in range(columns):

        @pl.when(pl.program_id(1) == shift)
        def _(shift=shift):
            out_ref[0] = (field_ref[0].astype(F32) + refs[shift][...].astype(F32)).astype(BF16)


def finish(probe, part, parts, place, field, pieces, previous):
    rows, channels, lanes = pieces[0].shape
    columns = len(pieces)
    step = 16 if rows % 16 == 0 else 8

    def where(n, shift, place_ref):
        block = lax.rem(place_ref[0] - shift + columns, columns)
        return (probe, n, 0, block * parts + part)

    block = pl.BlockSpec((1, step, channels, lanes), where)
    piece = pl.BlockSpec((step, channels, lanes), lambda n, shift, place_ref: (n, 0, 0))
    operands = [place, field, *pieces]
    specs = [block] + [piece] * columns
    aliases = {}
    if previous is not None:
        aliases = {len(operands): 0}
        operands.append(previous)
        specs.append(pl.BlockSpec(memory_space=pl.ANY))
    return pl.pallas_call(
        functools.partial(finish_kernel, columns),
        grid_spec=pltpu.PrefetchScalarGridSpec(
            num_scalar_prefetch=1,
            grid=(rows // step, columns),
            in_specs=specs,
            out_specs=block,
        ),
        out_shape=jax.ShapeDtypeStruct(field.shape, BF16),
        input_output_aliases=aliases,
        compiler_params=pltpu.CompilerParams(vmem_limit_bytes=VMEM_BYTES),
        cost_estimate=pl.CostEstimate(
            flops=rows * channels * lanes * columns,
            bytes_accessed=6 * rows * channels * lanes * columns,
            transcendentals=0,
        ),
    )(*operands)


def pick_kernel(row_ref, col_ref, field_ref, *refs):
    part_refs, out_ref = refs[:-1], refs[-1]
    fields, rows, lanes = field_ref.shape
    cells = row_ref.shape[1]
    chosen = lax.broadcasted_iota(jnp.int32, (rows, cells), 0) == row_ref[...]
    chosen = jnp.where(chosen, 1.0, 0.0).astype(BF16)
    column = lax.broadcasted_iota(jnp.int32, (lanes, cells), 0) == col_ref[...]
    for field in range(fields):
        update = jnp.concatenate([part_ref[field] for part_ref in part_refs], axis=1)
        tile = (field_ref[field].astype(F32) + update).astype(BF16)
        lines = lax.dot_general(
            tile, chosen, (((0,), (0,)), ((), ())), preferred_element_type=F32
        )
        picked = jnp.sum(jnp.where(column, lines, 0.0), axis=0, keepdims=True).astype(BF16)
        count = out_ref.shape[2]
        for band in range(out_ref.shape[0]):
            out_ref[band, field : field + 1] = picked[
                :, band * count : (band + 1) * count
            ]


def pick_cells(row, col, field, parts, bands):
    cells = row.shape[1]
    fields = field.shape[0]
    operands = (row, col, field, *parts)
    return call(
        pick_kernel,
        (1,),
        [whole_spec(operand) for operand in operands],
        pl.BlockSpec((bands, fields, cells // bands), lambda _: (0, 0, 0)),
        jax.ShapeDtypeStruct((bands, fields, cells // bands), BF16),
        4 * field.size * cells,
        8 * field.size,
    )(*operands)


def regrid_kernel(slot_ref, weight_ref, high_ref, low_ref):
    slots = high_ref.shape[1]
    lanes = high_ref.shape[2]
    number = lax.broadcasted_iota(jnp.int32, (slots, lanes), 0)
    total = jnp.zeros((slots, lanes), F32)
    for source in range(slot_ref.shape[1]):
        total = total + jnp.where(
            number == slot_ref[0, source : source + 1], weight_ref[0, source : source + 1], 0.0
        )
    high = total.astype(BF16)
    high_ref[0] = high
    low_ref[0] = (total - high.astype(F32)).astype(BF16)


def regrid_matrix(slot, weight, slots):
    rows, sources, lanes = slot.shape
    line = pl.BlockSpec((1, sources, lanes), lambda y: (y, 0, 0))
    table = pl.BlockSpec((1, slots, lanes), lambda y: (y, 0, 0))
    shape = jax.ShapeDtypeStruct((rows, slots, lanes), BF16)
    return call(
        regrid_kernel,
        (rows,),
        [line, line],
        [table, table],
        [shape, shape],
        12 * rows * slots * lanes,
        4 * rows * slots * lanes,
    )(slot, weight)


def start_kernel(pool_ref, high_ref, low_ref, coupling_ref, probe_ref, mask_ref, out_ref):
    pool = jnp.concatenate([pool_ref[band] for band in range(pool_ref.shape[0])], axis=1)
    flux = dot(pool, high_ref[0]) + dot(pool, low_ref[0])
    coupling = coupling_ref[...]
    fields = coupling.shape[1]
    for probe in range(probe_ref.shape[0]):
        total = probe_ref[probe, 0].astype(F32)
        for field in range(fields):
            line = probe * fields + field
            total = total + coupling[:, field : field + 1] * flux[line : line + 1]
        out_ref[probe, 0] = (total * mask_ref[0]).astype(BF16)


def start_level(pool, high, low, coupling, probe, mask):
    probes, rows, channels, lanes = probe.shape
    slots = high.shape[1]
    table = pl.BlockSpec((1, slots, lanes), lambda y: (y, 0, 0))
    line = pl.BlockSpec((probes, 1, channels, lanes), lambda y: (0, y, 0, 0))
    return call(
        start_kernel,
        (rows,),
        [
            whole_spec(pool),
            table,
            table,
            whole_spec(coupling),
            line,
            pl.BlockSpec((1, 1, lanes), lambda y: (y, 0, 0)),
        ],
        line,
        jax.ShapeDtypeStruct(probe.shape, BF16),
        32 * high.size,
        4 * high.size,
    )(pool, high, low, coupling, probe, mask)


def fill_padded(padded_ref, field_ref, top_ref, bottom_ref, left_ref, right_ref):
    rows, channels, lanes = field_ref.shape[1:]
    empty = jnp.zeros((channels, 122), F32)
    for line in range(rows + 6):
        if line < 3:
            inner = top_ref[0, line]
        elif line < rows + 3:
            inner = field_ref[0, line - 3]
        else:
            inner = bottom_ref[0, line - rows - 3]
        padded_ref[line, :, :lanes] = inner.astype(F32)
        padded_ref[line, :, lanes:] = jnp.concatenate(
            [right_ref[0, line].astype(F32), empty, left_ref[0, line].astype(F32)], axis=1
        )


def spread_rows(padded_ref, taps_ref, spread_ref):
    rows, channels, lanes = spread_ref.shape
    tiles = padded_ref.shape[2] // 128

    def step(index, carry):
        span = pl.ds(pl.multiple_of(index * 8, 8), 8)
        taps = taps_ref[span, :]
        totals = [jnp.zeros((8, lanes), F32) for _ in range(rows)]
        for right in range(7):
            sums = [[None] * tiles for _ in range(rows)]
            weights = [
                jnp.broadcast_to(taps[:, down * 7 + right : down * 7 + right + 1], (8, 128))
                for down in range(7)
            ]
            for line in range(rows + 6):
                for tile in range(tiles):
                    value = padded_ref[line, span, tile * 128 : (tile + 1) * 128]
                    for down in range(7):
                        row = line - down
                        if 0 <= row < rows:
                            term = value * weights[down]
                            held = sums[row][tile]
                            sums[row][tile] = term if held is None else held + term
                row = line - 6
                if row >= 0:
                    whole = jnp.concatenate(sums[row], axis=1)
                    if right != 3:
                        whole = pltpu.roll(whole, (3 - right) % (tiles * 128), 1)
                    totals[row] = totals[row] + whole[:, :lanes]
        for row in range(rows):
            spread_ref[row, span, :] = totals[row]
        return carry

    lax.fori_loop(0, channels // 8, step, 0)


def tangent_row(spread, base, scale, count):
    center = jnp.sum(spread, axis=0, keepdims=True) / count
    along = jnp.sum(base * spread, axis=0, keepdims=True) / count
    return (scale * (spread - center - base * along)).astype(BF16)


def split_dot(left, right):
    high = right.astype(BF16)
    low = (right - high.astype(F32)).astype(BF16)
    return dot(left, high) + dot(left, low)


def fine_kernel(
    field_ref,
    top_ref,
    bottom_ref,
    left_ref,
    right_ref,
    taps_ref,
    base_ref,
    sigma_ref,
    slope_ref,
    gain_ref,
    expand_ref,
    shrink_ref,
    down_ref,
    pairs_ref,
    mask_ref,
    level_ref,
    coarse_ref,
    padded_ref,
    spread_ref,
):
    first = pl.program_id(1) * 2
    channels = field_ref.shape[2]

    @pl.when(pl.program_id(1) == 0)
    def _():
        fill_padded(padded_ref, field_ref, top_ref, bottom_ref, left_ref, right_ref)
        spread_rows(padded_ref, taps_ref, spread_ref)

    pooled = None
    for slot in range(2):
        tangent = tangent_row(
            spread_ref[first + slot],
            base_ref[slot].astype(F32),
            gain_ref[...] * sigma_ref[slot],
            channels,
        )
        hidden = dot(expand_ref[...], tangent)
        gated = (slope_ref[slot].astype(F32) * hidden).astype(BF16)
        output = dot(shrink_ref[...], gated)
        field = field_ref[0, first + slot].astype(F32)
        level = ((field + output) * mask_ref[slot]).astype(BF16)
        level_ref[0, slot] = level
        share = dot(level, pairs_ref[...])
        pooled = share if pooled is None else pooled + share
    coarse_ref[0, 0] = split_dot(down_ref[...], pooled).astype(BF16)


def fine_level(field, sides, taps, base, sigma, slope, gain, expand, shrink, down, pairs, mask):
    probes, rows, channels, lanes = field.shape
    hidden = slope.shape[1]
    wide = down.shape[0]

    def of_probe(array):
        return pl.BlockSpec((1, *array.shape[1:]), lambda p, y: (p, 0, 0, 0))

    line = pl.BlockSpec((2, channels, lanes), lambda p, y: (y, 0, 0))
    thin = pl.BlockSpec((2, 1, lanes), lambda p, y: (y, 0, 0))
    return call(
        fine_kernel,
        (probes, rows // 2),
        [of_probe(field)]
        + [of_probe(side) for side in sides]
        + [
            whole_spec(taps),
            line,
            thin,
            pl.BlockSpec((2, hidden, lanes), lambda p, y: (y, 0, 0)),
            whole_spec(gain),
            whole_spec(expand),
            whole_spec(shrink),
            whole_spec(down),
            whole_spec(pairs),
            thin,
        ],
        [
            pl.BlockSpec((1, 2, channels, lanes), lambda p, y: (p, y, 0, 0)),
            pl.BlockSpec((1, 1, wide, lanes // 2), lambda p, y: (p, y, 0, 0)),
        ],
        [
            jax.ShapeDtypeStruct(field.shape, BF16),
            jax.ShapeDtypeStruct((probes, rows // 2, wide, lanes // 2), BF16),
        ],
        8 * probes * rows * lanes * channels * hidden,
        4 * slope.size + 8 * field.size,
        scratch=[
            pltpu.VMEM((rows + 6, channels, lanes + 128), F32),
            pltpu.VMEM((rows, channels, lanes), F32),
        ],
    )(field, *sides, taps, base, sigma, slope, gain, expand, shrink, down, pairs, mask)


def coarse_kernel(
    count,
    field_ref,
    top_ref,
    bottom_ref,
    left_ref,
    right_ref,
    level_ref,
    taps_ref,
    base_ref,
    sigma_ref,
    slope_ref,
    gain_ref,
    expand_ref,
    shrink_ref,
    up_ref,
    copies_ref,
    mask_ref,
    out_ref,
    padded_ref,
    spread_ref,
):
    _, rows, _, lanes = field_ref.shape
    fill_padded(padded_ref, field_ref, top_ref, bottom_ref, left_ref, right_ref)
    spread_rows(padded_ref, taps_ref, spread_ref)
    tangent = jnp.concatenate(
        [
            tangent_row(
                spread_ref[row],
                base_ref[row].astype(F32),
                gain_ref[...] * sigma_ref[row],
                count,
            )
            for row in range(rows)
        ],
        axis=1,
    )
    hidden = dot(expand_ref[...], tangent)
    gated = jnp.concatenate(
        [
            (slope_ref[row].astype(F32) * hidden[:, row * lanes : (row + 1) * lanes]).astype(BF16)
            for row in range(rows)
        ],
        axis=1,
    )
    output = dot(shrink_ref[...], gated)
    for row in range(rows):
        level = (
            field_ref[0, row].astype(F32) + output[:, row * lanes : (row + 1) * lanes]
        ).astype(BF16)
        raised = dot(up_ref[...], level)
        high = raised.astype(BF16)
        low = (raised - high.astype(F32)).astype(BF16)
        wide = dot(high, copies_ref[...]) + dot(low, copies_ref[...])
        for half in range(2):
            line = 2 * row + half
            total = (level_ref[0, line].astype(F32) + wide) * mask_ref[line]
            out_ref[0, line] = total.astype(BF16)


def coarse_level(count, field, sides, level, *constants):
    def of_probe(array):
        return pl.BlockSpec((1, *array.shape[1:]), lambda p: (p, 0, 0, 0))

    by_probe = (field, *sides, level)
    slope = constants[3]
    _, rows, channels, lanes = field.shape
    return call(
        functools.partial(coarse_kernel, count),
        (field.shape[0],),
        [of_probe(operand) for operand in by_probe]
        + [whole_spec(operand) for operand in constants],
        of_probe(level),
        jax.ShapeDtypeStruct(level.shape, BF16),
        8 * field.size * slope.shape[1],
        2 * slope.size + 4 * level.size,
        scratch=[
            pltpu.VMEM((rows + 6, channels, lanes + 128), F32),
            pltpu.VMEM((rows, channels, lanes), F32),
        ],
    )(*by_probe, *constants)


def widen(array, dim, size):
    pads = [(0, 0)] * array.ndim
    pads[dim] = (0, size - array.shape[dim])
    return jnp.pad(array, pads)


def local(
    probe_field,
    gate_slope,
    spectral_filter,
    weight_in,
    weight_out,
    weight_flux,
    send_cells,
    recv_slots,
    recv_weights,
    ocean_probe,
    ocean_mask,
    coupling,
    base_fine,
    sigma_fine,
    slope_fine,
    gain_fine,
    kernel_fine,
    expand_fine,
    shrink_fine,
    down_proj,
    base_coarse,
    sigma_coarse,
    slope_coarse,
    gain_coarse,
    kernel_coarse,
    expand_coarse,
    shrink_coarse,
    up_proj,
):
    probes, rows, width, lon_count = probe_field.shape
    lat_devices = lax.axis_size("lat")
    columns = lax.axis_size("chan")
    lat_place = lax.axis_index("lat")
    place = lax.axis_index("chan")
    channels = width * columns
    group = width // lat_devices
    lon_block = lon_count // columns
    lanes = min(128, lon_block)
    parts = lon_block // lanes
    fluxes = weight_flux.shape[1]

    fwd_lat, inv_lat = cosine_tables(rows * lat_devices)
    fwd_rows, inv_rows = fwd_lat.T, inv_lat.T
    filters = lax.dynamic_slice_in_dim(spectral_filter, lat_place * group, group, 1).T[:, :, None]
    win = (
        weight_in.reshape(columns, lat_devices, group, -1)
        .transpose(3, 1, 0, 2)
        .reshape(-1, channels)
    )
    wout = jnp.roll(weight_out.T, -place * width, axis=0)
    wflux = jnp.roll(weight_flux.T, -place * width, axis=1)
    flux_rows = lax.dynamic_slice_in_dim(weight_flux, place * width, width, 0)

    flux_share = jnp.einsum(
        "pncx,cf->pfnx", probe_field, flux_rows, preferred_element_type=F32
    ).astype(BF16)
    flux_share = flux_share.reshape(probes * fluxes * rows, columns, lon_block).transpose(1, 0, 2)
    flux_field = lax.psum_scatter(flux_share, "chan", scatter_dimension=0, tiled=False)
    flux_field = flux_field.reshape(probes, fluxes, rows, lon_block)

    tile_rows, tile_cols = ocean_probe.shape[2:]
    slots = lat_devices * send_cells.shape[2]
    cells = send_cells.reshape(1, -1)
    cell_row, cell_col = cells // lon_block, cells % lon_block
    sources = recv_slots.shape[1]
    regrid_high, regrid_low = regrid_matrix(
        recv_slots.reshape(sources, tile_rows, tile_cols).transpose(1, 0, 2),
        recv_weights.reshape(sources, tile_rows, tile_cols).transpose(1, 0, 2),
        slots,
    )
    mask = ocean_mask.astype(F32)[:, None, :]
    ocean_start = ocean_probe.transpose(0, 2, 1, 3)
    coupling_rows = coupling.T.astype(F32)
    fine_count = kernel_fine.shape[0]
    coarse_count = kernel_coarse.shape[0]
    wide = -(-coarse_count // 64) * 64
    fine_args = (
        kernel_fine,
        base_fine.transpose(1, 0, 2),
        sigma_fine[:, None, :],
        slope_fine.transpose(1, 0, 2),
        gain_fine[:, None],
        expand_fine.T,
        shrink_fine.T,
        widen(down_proj.T, 0, wide),
    )
    column = jnp.arange(tile_cols)
    pairs = jnp.where(column[:, None] // 2 == jnp.arange(tile_cols // 2)[None, :], 0.25, 0.0)
    pairs = pairs.astype(BF16)
    copies = jnp.where(jnp.arange(tile_cols // 2)[:, None] == column[None, :] // 2, 1.0, 0.0)
    copies = copies.astype(BF16)
    coarse_args = (
        widen(kernel_coarse, 0, wide),
        widen(base_coarse.transpose(1, 0, 2), 1, wide),
        sigma_coarse[:, None, :],
        slope_coarse.transpose(1, 0, 2),
        widen(gain_coarse[:, None], 0, wide),
        widen(expand_coarse.T, 1, wide),
        widen(shrink_coarse.T, 0, wide),
        widen(up_proj.T, 1, wide),
        copies,
    )

    def exchange(block, axes):
        return lax.all_to_all(block, axes, split_axis=0, concat_axis=0, tiled=True)

    def send_update(mixed, part):
        mixed = mixed.reshape(channels, rows, -1).transpose(1, 0, 2)
        flux, *pieces = network(mixed, gate_slope, part, win, wout, wflux, columns)
        arrived = [pieces[0]]
        for shift in range(1, columns):
            pairs_of = [(source, (source + shift) % columns) for source in range(columns)]
            arrived.append(lax.ppermute(pieces[shift], "chan", pairs_of))
        return flux, arrived

    prepared = (
        flux_field,
        regrid_high,
        regrid_low,
        mask,
        ocean_start,
        coupling_rows,
        fine_args,
        coarse_args,
        pairs,
        win,
        wout,
        wflux,
        cell_row,
        cell_col,
    )
    parts_of = [1] * (probes - 1) + [parts]
    place_word = place.astype(jnp.int32).reshape(1)

    def gather(probe, *others):
        block = turn(probe_field, probe).reshape(lat_devices, group, rows, lon_count)
        return exchange(tie(block, *others) if others else block, "lat")

    def mix(probe, part, gathered):
        return mix_latitudes(
            gathered, fwd_rows, inv_rows, filters, columns, part, parts_of[probe]
        )

    def give_back(mixed, *others):
        return exchange(tie(mixed, *others), ("lat", "chan"))

    def pick(probe, updates):
        fluxes_of = [update[0] for update in updates]
        return pick_cells(cell_row, cell_col, flux_field[probe], fluxes_of, lat_devices)

    def begin(probe, pool):
        return start_level(
            pool,
            regrid_high,
            regrid_low,
            coupling_rows,
            ocean_start[probe : probe + 1],
            mask,
        )

    def fine(start, ends, *others):
        left, right = halo_columns(start, *ends)
        if others:
            left = tie(left, *others)
        return fine_level(start, (*ends, left, right), *fine_args, pairs, mask)

    def coarse(level, field, *others):
        ends = halo_rows(field)
        left, right = halo_columns(field, *ends)
        if others:
            left = tie(left, *others)
        sides = (*ends, left, right)
        out = coarse_level(coarse_count, field, sides, level, *coarse_args, mask)
        return out[0].transpose(1, 0, 2)

    def finish_all(probe, updates, atmos_out):
        for part, update in enumerate(updates):
            atmos_out = finish(
                probe, part, len(updates), place_word, probe_field, update[1], atmos_out
            )
        return atmos_out

    atmos_out = None
    gathered = gather(0)
    ahead = [prepared, flux_share]
    for probe in range(probes - 1):
        mixed = mix(probe, 0, gathered)
        arrived = give_back(mixed, gathered, ahead)
        gathered = gather(probe + 1, arrived)
        updates = [send_update(arrived, 0)]
        pool = lax.all_gather(pick(probe, updates), "lat", axis=0, tiled=False)
        pool = lax.dynamic_index_in_dim(pool, lat_place, 1, keepdims=False)
        start = begin(probe, pool)
        atmos_out = finish_all(probe, updates, atmos_out)
        ends = halo_rows(start)
        ahead = [ends, atmos_out]

    results = []
    probe = probes - 1
    arrived = [give_back(mix(probe, 0, gathered), gathered, ahead)]
    level, low = fine(start, ends)
    for part in range(1, parts):
        arrived.append(give_back(mix(probe, part, gathered), arrived[-1], low))
    updates = [send_update(arrived[part], part) for part in range(parts - 1)]
    before = [update[0] for update in updates]
    updates.append(send_update(tie(arrived[-1], before), parts - 1))
    pool = exchange(pick(probe, updates), "lat")
    results.append(coarse(level, tie(low, updates[-1][0])))
    back = [update[1] for update in updates[:-1]]
    start = begin(probe, tie(pool, back) if back else pool)
    level, low = fine(start, halo_rows(start))
    results.append(coarse(level, low, updates[-1][1], results[0]))
    atmos_out = finish_all(probe, updates, atmos_out)
    return (atmos_out, jnp.stack(results))


def solution(mesh):
    return jax.shard_map(
        local,
        mesh=mesh,
        in_specs=(
            P(None, "lat", "chan", None),
            P("lat", None, "chan"),
            P(None, "chan"),
            P(),
            P(),
            P(),
            P(("lat", "chan"), None, None),
            P(("lat", "chan"), None, None),
            P(("lat", "chan"), None, None),
            P(None, None, "lat", "chan"),
            P("lat", "chan"),
            P(),
            P(None, "lat", "chan"),
            P("lat", "chan"),
            P(None, "lat", "chan"),
            P(),
            P(),
            P(),
            P(),
            P(),
            P(None, "lat", "chan"),
            P("lat", "chan"),
            P(None, "lat", "chan"),
            P(),
            P(),
            P(),
            P(),
            P(),
        ),
        out_specs=(P(None, "lat", "chan", None), P(None, None, "lat", "chan")),
        check_vma=False,
    )
```
